32 devices in a mesh: dp: 4 (over x, core), patch: 8 (over z, y).
Axes of the slice: x: 2, y: 2, z: 4, core: 2. Of those that a mesh axis runs over, the one named last changes fastest.
Arguments:
- rows: bfloat16 [22528, 1280], P(('dp', 'patch')), may hold values from -6 to 6
- grad_hidden: bfloat16 [22528, 2560], P(('dp', 'patch')), may hold values from -6 to 6
- counts: int32 [4, 8], P('dp'), may hold values from 1 to 704, 2816 in all within a row
- w_in: bfloat16 [2560, 1280], P('patch'), may hold values from -0.15625 to 0.15625
- b_in: bfloat16 [2560], P('patch'), may hold values from -3 to 3
- gamma: float32 [1280], replicated, may hold values from 0.1 to 1.9
- beta: float32 [1280], replicated, may hold values from -3 to 3
Outputs:
- grad_rows: bfloat16 [22528, 1280], P(('dp', 'patch'))
- grad_w_in: float32 [2560, 1280], P('patch')
The draws below stay inside these ranges and needn't reach their ends.
Inputs may be any that keep to these rules, and one draw needn't show every extreme that they name: In each dp group the 8 counts sum to 2816, and one device of each group has exactly 704.
All inputs are finite; a program needn't handle non-finite values.
Results may differ from the reference program's by a relative error of at most 0.0056.
Values may be sent and summed in bfloat16 or wider, within the bound.
No kernel may reach another device: no remote copies, remote signals or barrier semaphores. Data moves between devices by JAX's collectives and lax.ppermute only.
A program may use at most 128 MiB of HBM per device.

```python
import math
import jax
import jax.numpy as jnp
import numpy as np
from jax import lax

D = 1280
FF = 2560
VIS_DEV = 352
P_DEV = 704
ROWS_ALL = 22528
N_DP = 4
N_PATCH = 8


def block_levels(stream_key, shape, split, low, largest):
    gain, own = 1.0, jax.random.fold_in(stream_key, 6)
    for axis_at, parts in split:
        steps = jnp.exp(jax.random.uniform(jax.random.fold_in(own, axis_at), (parts,), jnp.float32, low / len(split), largest / len(split)))
        gain = gain * jnp.repeat(steps, shape[axis_at] // parts).reshape([-1 if axis == axis_at else 1 for axis in range(len(shape))])
    return gain


def profile(amount, total, bound, lean):
    loads = [(1 << 20) // math.isqrt(grade ** lean) + 1 for grade in range(2, amount + 1)]
    spare, holding = total - bound - (amount - 1), [1] * (amount - 1)
    while spare > 0:
        movable = [i for i in range(amount - 1) if holding[i] < bound]
        mass, left = sum([loads[i] for i in movable]), spare
        for i in movable:
            addition = min(bound - holding[i], max(1, left * loads[i] // mass), spare)
            holding[i] = holding[i] + addition
            spare = spare - addition
    return np.array([bound] + holding)


def uneven(key, amount, total, bound, slope):
    if amount == 2:
        one = jax.random.randint(key, (), max(1, total - bound), min(bound, total - 1) + 1)
        return jnp.stack([one, total - one])
    tallies = jnp.asarray(profile(amount, total, bound, slope), jnp.int32)
    couples = (amount - 1) // 2
    giver, sink = tallies[1:1 + 2 * couples:2], tallies[2:2 + 2 * couples:2]
    slack = jnp.minimum(giver - 1, bound - sink)
    moved = jax.random.randint(jax.random.fold_in(key, 1), (couples,), 0, 1 << 20) % (slack + 1)
    tallies = tallies.at[1:1 + 2 * couples:2].set(giver - moved).at[2:2 + 2 * couples:2].set(sink + moved)
    return tallies[jax.random.permutation(jax.random.fold_in(key, 2), amount)]


def normal_values(rng, dims, width, bound, cuts=(), kind=jnp.bfloat16):
    factor_of = block_levels(rng, dims, cuts, -0.22, 0.18) if cuts else 1.0
    result = jax.random.normal(rng, dims, jnp.float32) * width * factor_of
    return jnp.minimum(jnp.maximum(result, -bound), bound).astype(kind)


def setup_inputs(seed: int = 0) -> dict:
    keys = jax.random.split(jax.random.key(seed), 8)
    rows = normal_values(keys[0], (ROWS_ALL, D), 1.0, 6.0, ((0, 32),))
    grad_hidden = normal_values(keys[1], (ROWS_ALL, FF), 1.0, 6.0, ((0, 32),))
    counts = jax.vmap(lambda own: uneven(own, N_PATCH, VIS_DEV * N_PATCH, P_DEV, 2))(jax.random.split(keys[2], N_DP)).reshape((N_DP, N_PATCH)).astype(jnp.int32)
    w_in = normal_values(keys[3], (FF, D), D ** -0.5, 0.15625, ((0, 8),))
    b_in = normal_values(keys[4], (FF,), 0.5, 3.0, ((0, 8),))
    gamma = jnp.clip(1.0 + 0.18 * jax.random.normal(keys[5], (D,), jnp.float32), 0.1, 1.9)
    beta = normal_values(keys[6], (D,), 0.5, 3.0, (), jnp.float32)
    return {"rows": rows, "grad_hidden": grad_hidden, "counts": counts, "w_in": w_in, "b_in": b_in, "gamma": gamma, "beta": beta}


def gelu_slope(pre_act):
    normal_cdf = 0.5 * (1.0 + jax.scipy.special.erf(pre_act * (1.0 / math.sqrt(2.0))))
    density = jnp.exp(-0.5 * pre_act * pre_act) * (1.0 / math.sqrt(2.0 * math.pi))
    return normal_cdf + pre_act * density

def normed(block, gamma, beta):
    as_float = block.astype(jnp.float32)
    mean_row = lax.optimization_barrier(jnp.mean(as_float, axis=1, keepdims=True))
    centred = as_float - mean_row
    variance = lax.optimization_barrier(jnp.mean(centred * centred, axis=1, keepdims=True))
    inverse = lax.rsqrt(variance + 1e-05)
    standard = centred * inverse
    normed_rows = (standard * gamma + beta).astype(jnp.bfloat16)
    return (standard, inverse, normed_rows)

def finish(normed_grad, standard, inverse, gamma):
    scaled = normed_grad * gamma
    first = lax.optimization_barrier(jnp.mean(scaled, axis=1, keepdims=True))
    second = lax.optimization_barrier(jnp.mean(scaled * standard, axis=1, keepdims=True))
    return inverse * (scaled - first - standard * second)

def reference(rows, grad_hidden, counts, w_in, b_in, gamma, beta):
    model_width = rows.shape[1]
    hidden_units = grad_hidden.shape[1]
    per_dev = rows.shape[0] // (N_DP * N_PATCH)
    group_rows = VIS_DEV * N_PATCH
    scene_rows = rows.reshape(N_DP, N_PATCH * per_dev, model_width)
    scene_grads = grad_hidden.reshape(N_DP, N_PATCH * per_dev, hidden_units)
    positions = jnp.arange(group_rows, dtype=jnp.int32)

    def one_group(running, packet):
        group_x, group_g, row_counts = packet
        offsets = (jnp.cumsum(row_counts) - row_counts).astype(jnp.int32)
        source = (lax.optimization_barrier(jnp.sum((offsets[None, :] <= positions[:, None]).astype(jnp.int32), axis=1)) - 1).astype(jnp.int32)
        placement = (source * per_dev + positions - jnp.take(offsets, source)).astype(jnp.int32)
        picked_x = jnp.take(group_x, placement, axis=0)
        picked_g = jnp.take(group_g, placement, axis=0)
        standard, inverse, normed_rows = normed(picked_x, gamma, beta)
        pre_act = lax.dot_general(normed_rows, w_in, (((1,), (1,)), ((), ())), preferred_element_type=jnp.float32) + b_in.astype(jnp.float32)
        hidden_grad = (picked_g.astype(jnp.float32) * gelu_slope(pre_act)).astype(jnp.bfloat16)
        normed_grad = jnp.dot(hidden_grad, w_in, preferred_element_type=jnp.float32)
        grad_here = finish(normed_grad, standard, inverse, gamma).astype(jnp.bfloat16)
        scattered = jnp.zeros(group_x.shape, jnp.bfloat16).at[placement].set(grad_here)
        grad_term = lax.dot_general(hidden_grad, normed_rows, (((0,), (0,)), ((), ())), preferred_element_type=jnp.float32)
        return (running + grad_term, scattered)
    initial = jnp.zeros((hidden_units, model_width), jnp.float32)
    running, scattered = lax.scan(one_group, initial, (scene_rows, scene_grads, counts))
    grad_scale = 1.0 / math.sqrt(VIS_DEV * N_PATCH * N_DP)
    return (scattered.reshape(rows.shape), running * grad_scale)
```

```python
import functools
import math

import jax
import jax.numpy as jnp
import numpy as np
from jax import lax
from jax.experimental import pallas as pl
from jax.experimental.pallas import tpu as pltpu
from jax.sharding import PartitionSpec as P

VIS_DEV = 352
AXES = ("dp", "patch")
F32, BF16 = jnp.float32, jnp.bfloat16
VMEM = pl.BlockSpec(memory_space=pltpu.VMEM)
SMEM = pl.BlockSpec(memory_space=pltpu.SMEM)
LIMIT = 56 * 1024 * 1024


def gelu_slope(pre_act):
    normal_cdf = 0.5 * (1.0 + lax.erf(pre_act * (1.0 / math.sqrt(2.0))))
    density = jnp.exp(-0.5 * pre_act * pre_act) * (1.0 / math.sqrt(2.0 * math.pi))
    return normal_cdf + pre_act * density


def standardise(block):
    as_float = block.astype(F32)
    mean_row = jnp.mean(as_float, axis=1, keepdims=True)
    centred = as_float - mean_row
    variance = jnp.mean(centred * centred, axis=1, keepdims=True)
    inverse = lax.rsqrt(variance + 1e-05)
    return centred * inverse, inverse


def norm_kernel(rows_ref, gamma_ref, beta_ref, out_ref):
    standard, _ = standardise(rows_ref[...])
    out_ref[...] = (standard * gamma_ref[...] + beta_ref[...]).astype(BF16)


def chunk_kernel(places, pieces, table_ref, counts_ref, n_ref, g_ref, b_ref, *refs):
    piece_refs, (keep_ref, send_ref, h_ref, w_ref), (sum_ref,) = refs[:pieces], refs[pieces : pieces + 4], refs[pieces + 4 :]
    for at, piece in enumerate(piece_refs):
        start = pl.multiple_of(table_ref[places["pieces"] + at], 16)
        w_ref[pl.ds(start, piece.shape[0]), :] = piece[...]
    per_dev, units = h_ref.shape
    count = counts_ref[0, table_ref[places["patch"]]]
    live = lax.broadcasted_iota(jnp.int32, (per_dev, 1), 0) < count
    for low in range(0, units, 256):
        cols = slice(low, min(low + 256, units))
        pre_act = lax.dot_general(n_ref[...], w_ref[cols, :], (((1,), (1,)), ((), ())), preferred_element_type=F32)
        slope = gelu_slope(pre_act + b_ref[:, cols].astype(F32))
        hidden = jnp.where(live, g_ref[:, cols].astype(F32) * slope, 0.0)
        h_ref[:, cols] = hidden.astype(BF16)
    width = n_ref.shape[1]
    block = keep_ref.shape[0] // 4
    for low in range(0, width, 256):
        cols = slice(low, min(low + 256, width))
        sum_ref[:, cols] = lax.dot_general(
            h_ref[...], n_ref[:, cols], (((0,), (0,)), ((), ())), preferred_element_type=F32
        )
    for at in range(8):
        start = pl.multiple_of(table_ref[places["blocks"] + at], 16)
        out = send_ref if at < 4 else keep_ref
        out[(at % 4) * block : (at % 4 + 1) * block, :] = sum_ref[pl.ds(start, block), :].astype(BF16)


def rows_kernel(places, chunks, table_ref, counts_ref, rows_ref, gamma_ref, *refs):
    h_refs, w_refs, out_ref = refs[:chunks], refs[chunks : 2 * chunks], refs[-1]
    tile = rows_ref.shape[0]
    normed_grad = jnp.dot(h_refs[0][...], w_refs[0][...], preferred_element_type=F32)
    for h, w in zip(h_refs[1:], w_refs[1:]):
        normed_grad += jnp.dot(h[...], w[...], preferred_element_type=F32)
    standard, inverse = standardise(rows_ref[...])
    scaled = normed_grad * gamma_ref[...]
    first = jnp.mean(scaled, axis=1, keepdims=True)
    second = jnp.mean(scaled * standard, axis=1, keepdims=True)
    grad = inverse * (scaled - first - standard * second)
    count = counts_ref[0, table_ref[places["patch"]]]
    row = lax.broadcasted_iota(jnp.int32, (tile, 1), 0) + pl.program_id(0) * tile
    out_ref[...] = jnp.where(row < count, grad, 0.0).astype(BF16)


def place_kernel(places, table_ref, *refs):
    quarter = refs[0].shape[0]
    for at, piece in enumerate(refs[:-1]):
        start = pl.multiple_of(table_ref[places["final"] + at], 16)
        refs[-1][pl.ds(start, quarter), :] = piece[...].astype(F32)


class Plan:
    def __init__(self, n_dp, n_patch, shard):
        self.nz, self.ny, self.nx = n_patch // 2, 2, 2
        self.n_patch, self.shard, self.quarter = n_patch, shard, shard // 4
        self.everyone = [
            (x, c, z, y) for x in range(2) for c in range(2) for z in range(self.nz) for y in range(2)
        ]

    def lin(self, x, c, z, y):
        return ((x * 2 + c) * self.nz + z) * 2 + y

    def perm(self, to):
        return [(self.lin(*d), self.lin(*to(*d))) for d in self.everyone]

    def across(self, x, c, z, y, flip_x, flip_y):
        return (x ^ flip_x, c, z, y ^ flip_y)

    def first(self, x, c, z, y):
        return (1 - x, c, z, y) if c == 0 else (x, c, z, 1 - y)

    def second(self, x, c, z, y):
        return (1 - x, c, z, y) if c == 1 else (x, c, z, 1 - y)

    def row(self, x, c, z, y):
        return y * self.shard + (x * 2 + c) * self.quarter

    def table(self):
        rows = []
        for d in self.everyone:
            x, c, z, y = d
            twin = (x, 1 - c, z, y)
            four = lambda e: [e, self.first(*e), self.second(*e), self.second(*self.first(*e))]
            order = lambda e: [four(e)[i] for i in (3, 1, 2, 0)]
            entry = [z * 2 + y]
            entry += [(z - s) % self.nz for s in range(self.nz)]
            entry += [self.row(*e) for e in four(d) + four(twin)]
            entry += [y * self.shard] + [
                self.row(qx, qc, z, 1 - y) for qx, qc in ((x, c), (1 - x, c), (x, 1 - c), (1 - x, 1 - c))
            ]
            entry += [self.row(*e) for e in order(twin) + order(d)]
            entry += [
                self.row(qx, qc, z, 0) for qx, qc in ((x, c), (1 - x, c), (x, 1 - c), (1 - x, 1 - c))
            ]
            rows.append(entry)
        return np.array(rows, np.int32)

    def places(self):
        base = 1 + self.nz
        return {"patch": 0, "chunk": 1, "far": base, "near": base + 8, "blocks": base + 13, "final": base + 21}


def call_chunk(places, step, table, counts, normed_rows, grad_hidden, bias, pieces, shard, near):
    per_dev, width = normed_rows.shape
    units = 2 * shard
    where = dict(places, pieces=places["near" if near else "far"])
    whole = lambda shape: pl.BlockSpec(shape, lambda i, t, c: (0,) * len(shape))
    return pl.pallas_call(
        functools.partial(chunk_kernel, where, len(pieces)),
        grid_spec=pltpu.PrefetchScalarGridSpec(
            num_scalar_prefetch=2,
            grid=(1,),
            in_specs=[
                whole((per_dev, width)),
                pl.BlockSpec((per_dev, units), lambda i, t, c: (0, t[places["chunk"] + step])),
                whole((1, units)),
            ]
            + [whole(p.shape) for p in pieces],
            out_specs=[
                whole((units // 2, width)),
                whole((units // 2, width)),
                whole((per_dev, units)),
                whole((units, width)),
            ],
            scratch_shapes=[pltpu.VMEM((units, width), F32)],
        ),
        out_shape=[
            jax.ShapeDtypeStruct((units // 2, width), BF16),
            jax.ShapeDtypeStruct((units // 2, width), BF16),
            jax.ShapeDtypeStruct((per_dev, units), BF16),
            jax.ShapeDtypeStruct((units, width), BF16),
        ],
        compiler_params=pltpu.CompilerParams(vmem_limit_bytes=LIMIT),
        cost_estimate=pl.CostEstimate(
            flops=4 * per_dev * units * width,
            bytes_accessed=2 * per_dev * (width + 2 * units) + 6 * units * width,
            transcendentals=per_dev * units,
        ),
        name="chunk_%d" % step,
    )(table, counts, normed_rows, grad_hidden, bias, *pieces)


def fast_device(plan, rows, grad_hidden, counts, w_in, b_in, gamma, beta):
    per_dev, width = rows.shape
    shard, quarter = plan.shard, plan.quarter
    n_patch = plan.n_patch
    dp_index, patch_index = lax.axis_index("dp"), lax.axis_index("patch")
    places = plan.places()
    table = lax.dynamic_index_in_dim(
        jnp.asarray(plan.table()), dp_index * n_patch + patch_index, 0, keepdims=False
    )
    gamma, beta = gamma.reshape(1, width), beta.reshape(1, width)
    swap = lambda to: functools.partial(lax.ppermute, axis_name=AXES, perm=plan.perm(to))
    core = swap(lambda x, c, z, y: (x, 1 - c, z, y))
    along_x = swap(lambda x, c, z, y: (1 - x, c, z, y))
    along_y = swap(lambda x, c, z, y: (x, c, z, 1 - y))
    first, second = swap(plan.first), swap(plan.second)
    up = lambda s: swap(lambda x, c, z, y: (x, c, (z + s) % plan.nz, y))

    mine = lax.dynamic_slice_in_dim(w_in, dp_index * quarter, quarter, 0)
    from_z = [None] + [up(s)(mine) for s in range(1, plan.nz)]
    beside = along_y(mine)
    diagonal = along_x(beside)
    pieces = [[w_in, beside, diagonal, core(beside), core(diagonal)]]
    bias_mine = b_in.reshape(1, shard)
    bias_other = along_y(bias_mine)
    low = patch_index % 2 == 0
    bias_here = jnp.concatenate(
        [jnp.where(low, bias_mine, bias_other), jnp.where(low, bias_other, bias_mine)], axis=1
    )
    bias = [bias_here] + [up(s)(bias_here) for s in range(1, plan.nz)]
    for s in range(1, plan.nz):
        a0 = from_z[s]
        a1 = first(a0)
        a2, a3 = second(a0), second(a1)
        pieces.append([a0, a1, a2, a3] + [core(a) for a in (a0, a1, a2, a3)])

    tile = per_dev // 4
    normed_rows = pl.pallas_call(
        norm_kernel,
        grid=(per_dev // tile,),
        in_specs=[
            pl.BlockSpec((tile, width), lambda i: (i, 0)),
            pl.BlockSpec((1, width), lambda i: (0, 0)),
            pl.BlockSpec((1, width), lambda i: (0, 0)),
        ],
        out_specs=pl.BlockSpec((tile, width), lambda i: (i, 0)),
        out_shape=jax.ShapeDtypeStruct((per_dev, width), BF16),
        compiler_params=pltpu.CompilerParams(vmem_limit_bytes=LIMIT),
        name="norm",
    )(rows, gamma, beta)

    hidden, weights, total = [], [], None
    scale = 1.0 / math.sqrt(VIS_DEV * n_patch * 4)
    for s in range(plan.nz):
        keep, send, h, w = call_chunk(
            places, s, table, counts, normed_rows, grad_hidden, bias[s], pieces[s], shard, s == 0
        )
        hidden.append(h)
        weights.append(w)
        own = lambda low, high: keep[low:high].astype(F32) + got[low:high].astype(F32)
        got = core(send)
        one = first(own(0, 2 * quarter).astype(BF16))
        two = second((own(2 * quarter, 3 * quarter) + one[:quarter].astype(F32)).astype(BF16))
        plane = own(3 * quarter, 4 * quarter) + one[quarter:].astype(F32) + two.astype(F32)
        if s:
            plane = up(-s)(plane.astype(BF16)).astype(F32)
        total = plane if total is None else total + plane
    done = (total * scale).astype(BF16)
    done_x = along_x(done)
    quarters = [done, done_x, core(done), core(done_x)]
    grad_w_in = pl.pallas_call(
        functools.partial(place_kernel, places),
        in_specs=[SMEM] + [VMEM] * 4,
        out_specs=VMEM,
        out_shape=jax.ShapeDtypeStruct((shard, width), F32),
        name="place",
    )(table, *quarters)

    whole = lambda shape: pl.BlockSpec(shape, lambda i, t, c: (0,) * len(shape))
    striped = lambda cols: pl.BlockSpec((tile, cols), lambda i, t, c: (i, 0))
    grad_rows = pl.pallas_call(
        functools.partial(rows_kernel, places, plan.nz),
        grid_spec=pltpu.PrefetchScalarGridSpec(
            num_scalar_prefetch=2,
            grid=(per_dev // tile,),
            in_specs=[striped(width), whole((1, width))]
            + [striped(h.shape[1]) for h in hidden]
            + [whole(w.shape) for w in weights],
            out_specs=striped(width),
        ),
        out_shape=jax.ShapeDtypeStruct((per_dev, width), BF16),
        compiler_params=pltpu.CompilerParams(vmem_limit_bytes=LIMIT),
        cost_estimate=pl.CostEstimate(
            flops=2 * per_dev * width * 2 * shard * plan.nz,
            bytes_accessed=4 * per_dev * width + 2 * (per_dev + width) * 2 * shard * plan.nz,
            transcendentals=0,
        ),
        name="grad_rows",
    )(table, counts, rows, gamma, *hidden, *weights)
    return grad_rows, grad_w_in


def any_device(rows, grad_hidden, counts, w_in, b_in, gamma, beta):
    patch_count, data_count = lax.axis_size("patch"), lax.axis_size("dp")
    live = (jnp.arange(rows.shape[0], dtype=jnp.int32) < jnp.take(counts[0], lax.axis_index("patch")))[:, None]
    standard, inverse = standardise(rows)
    normed_rows = (standard * gamma + beta).astype(BF16)
    w_all = lax.all_gather(w_in, "patch", axis=0, tiled=True)
    b_all = lax.all_gather(b_in, "patch", axis=0, tiled=True)
    pre_act = lax.dot_general(normed_rows, w_all, (((1,), (1,)), ((), ())), preferred_element_type=F32)
    slope = gelu_slope(pre_act + b_all.astype(F32))
    hidden = jnp.where(live, grad_hidden.astype(F32) * slope, 0.0).astype(BF16)
    scaled = jnp.dot(hidden, w_all, preferred_element_type=F32) * gamma
    first = jnp.mean(scaled, axis=1, keepdims=True)
    second = jnp.mean(scaled * standard, axis=1, keepdims=True)
    grad = inverse * (scaled - first - standard * second)
    grad_rows = jnp.where(live, grad, 0.0).astype(BF16)
    term = lax.dot_general(hidden, normed_rows, (((0,), (0,)), ((), ())), preferred_element_type=F32)
    scale = 1.0 / math.sqrt(VIS_DEV * patch_count * data_count)
    part = lax.psum_scatter(term * scale, "patch", scatter_dimension=0, tiled=True)
    return grad_rows, lax.psum(part, "dp")


def solution(mesh):
    n_dp, n_patch = mesh.shape["dp"], mesh.shape["patch"]

    def per_device(*args):
        shard = args[3].shape[0]
        if n_dp == 4 and n_patch % 2 == 0 and n_patch <= 8 and shard % 64 == 0 and args[0].shape[0] % 64 == 0:
            return fast_device(Plan(n_dp, n_patch, shard), *args)
        return any_device(*args)

    in_specs = (
        P(AXES, None), P(AXES, None), P("dp", None), P("patch", None), P("patch"), P(), P(),
    )
    return jax.shard_map(
        per_device, mesh=mesh, in_specs=in_specs, out_specs=(P(AXES, None), P("patch", None)), check_vma=False
    )
```

```python
import functools
import math

import jax
import jax.numpy as jnp
import numpy as np
from jax import lax
from jax.experimental import pallas as pl
from jax.experimental.pallas import tpu as pltpu
from jax.sharding import PartitionSpec as P

VIS_DEV = 352
AXES = ("dp", "patch")
F32, BF16 = jnp.float32, jnp.bfloat16
VMEM = pl.BlockSpec(memory_space=pltpu.VMEM)
SMEM = pl.BlockSpec(memory_space=pltpu.SMEM)
LIMIT = 56 * 1024 * 1024


def gelu_slope(pre_act):
    normal_cdf = 0.5 * (1.0 + lax.erf(pre_act * (1.0 / math.sqrt(2.0))))
    density = jnp.exp(-0.5 * pre_act * pre_act) * (1.0 / math.sqrt(2.0 * math.pi))
    return normal_cdf + pre_act * density


def standardise(block):
    as_float = block.astype(F32)
    mean_row = jnp.mean(as_float, axis=1, keepdims=True)
    centred = as_float - mean_row
    variance = jnp.mean(centred * centred, axis=1, keepdims=True)
    inverse = lax.rsqrt(variance + 1e-05)
    return centred * inverse, inverse


def norm_kernel(rows_ref, gamma_ref, beta_ref, out_ref):
    standard, _ = standardise(rows_ref[...])
    out_ref[...] = (standard * gamma_ref[...].reshape(1, -1) + beta_ref[...].reshape(1, -1)).astype(BF16)


def chunk_kernel(places, pieces, waits, table_ref, counts_ref, n_ref, g_ref, b_ref, *refs):
    piece_refs, (keep_ref, *send_refs, h_ref, w_ref), (sum_ref,) = (
        refs[:pieces],
        refs[pieces + waits : pieces + waits + 5],
        refs[pieces + waits + 5 :],
    )
    block = keep_ref.shape[0] // 4
    bias = b_ref[...].astype(F32)
    for at, piece in enumerate(piece_refs):
        start = pl.multiple_of(table_ref[places["pieces"] + at], 16)
        extra = piece.shape[0] % block
        size = piece.shape[0] - extra
        w_ref[pl.ds(start, size), :] = piece[:size, :]
        if extra:
            bias += piece[size:, : bias.shape[1]].astype(F32)[:1]
    per_dev, units = h_ref.shape
    count = counts_ref[0, table_ref[places["patch"]]]
    live = lax.broadcasted_iota(jnp.int32, (per_dev, 1), 0) < count
    for low in range(0, units, 256):
        cols = slice(low, min(low + 256, units))
        pre_act = lax.dot_general(n_ref[...], w_ref[cols, :], (((1,), (1,)), ((), ())), preferred_element_type=F32)
        slope = gelu_slope(pre_act + bias[:, cols])
        hidden = jnp.where(live, g_ref[:, cols].astype(F32) * slope, 0.0)
        h_ref[:, cols] = hidden.astype(BF16)
    width = n_ref.shape[1]
    for low in range(0, width, 256):
        cols = slice(low, min(low + 256, width))
        sum_ref[:, cols] = lax.dot_general(
            h_ref[...], n_ref[:, cols], (((0,), (0,)), ((), ())), preferred_element_type=F32
        )
    for at in range(8):
        start = pl.multiple_of(table_ref[places["blocks"] + at], 16)
        out, to = (send_refs[at // 2], at % 2) if at < 4 else (keep_ref, at % 4)
        out[to * block : (to + 1) * block, :] = sum_ref[pl.ds(start, block), :].astype(BF16)


def rows_kernel(places, chunks, first_tile, table_ref, counts_ref, rows_ref, gamma_ref, *refs):
    h_refs, w_refs, out_ref = refs[:chunks], refs[chunks : 2 * chunks], refs[-1]
    tile = rows_ref.shape[0]
    normed_grad = jnp.dot(h_refs[0][...], w_refs[0][...], preferred_element_type=F32)
    for h, w in zip(h_refs[1:], w_refs[1:]):
        normed_grad += jnp.dot(h[...], w[...], preferred_element_type=F32)
    standard, inverse = standardise(rows_ref[...])
    scaled = normed_grad * gamma_ref[...].reshape(1, -1)
    first = jnp.mean(scaled, axis=1, keepdims=True)
    second = jnp.mean(scaled * standard, axis=1, keepdims=True)
    grad = inverse * (scaled - first - standard * second)
    count = counts_ref[0, table_ref[places["patch"]]]
    row = lax.broadcasted_iota(jnp.int32, (tile, 1), 0) + (pl.program_id(0) + first_tile) * tile
    out_ref[...] = jnp.where(row < count, grad, 0.0).astype(BF16)


def place_kernel(places, table_ref, *refs):
    quarter = refs[0].shape[0]
    for at, piece in enumerate(refs[:-1]):
        start = pl.multiple_of(table_ref[places["final"] + at], 16)
        refs[-1][pl.ds(start, quarter), :] = piece[...].astype(F32)


class Plan:
    def __init__(self, n_dp, n_patch, shard):
        self.nz, self.ny, self.nx = n_patch // 2, 2, 2
        self.n_patch, self.shard, self.quarter = n_patch, shard, shard // 4
        self.everyone = [
            (x, c, z, y) for x in range(2) for c in range(2) for z in range(self.nz) for y in range(2)
        ]

    def lin(self, x, c, z, y):
        return ((x * 2 + c) * self.nz + z) * 2 + y

    def perm(self, to):
        return [(self.lin(*d), self.lin(*to(*d))) for d in self.everyone]

    def across(self, x, c, z, y, flip_x, flip_y):
        return (x ^ flip_x, c, z, y ^ flip_y)

    def first(self, x, c, z, y):
        return (1 - x, c, z, y) if c == 0 else (x, c, z, 1 - y)

    def second(self, x, c, z, y):
        return (1 - x, c, z, y) if c == 1 else (x, c, z, 1 - y)

    def row(self, x, c, z, y):
        return y * self.shard + (x * 2 + c) * self.quarter

    def table(self):
        rows = []
        for d in self.everyone:
            x, c, z, y = d
            twin = (x, 1 - c, z, y)
            four = lambda e: [e, self.first(*e), self.second(*e), self.second(*self.first(*e))]
            order = lambda e: [four(e)[i] for i in (3, 1, 2, 0)]
            entry = [z * 2 + y]
            entry += [(z - s) % self.nz for s in range(self.nz)]
            entry += [self.row(*e) for e in four(d) + four(twin)]
            entry += [y * self.shard] + [
                self.row(qx, qc, z, 1 - y) for qx, qc in ((x, c), (1 - x, c), (x, 1 - c), (1 - x, 1 - c))
            ]
            entry += [self.row(*e) for e in order(twin) + order(d)]
            entry += [
                self.row(qx, qc, z, 0) for qx, qc in ((x, c), (1 - x, c), (x, 1 - c), (1 - x, 1 - c))
            ]
            rows.append(entry)
        return np.array(rows, np.int32)

    def places(self):
        base = 1 + self.nz
        return {"patch": 0, "chunk": 1, "far": base, "near": base + 8, "blocks": base + 13, "final": base + 21}


def call_chunk(places, step, table, counts, normed_rows, grad_hidden, bias, pieces, shard, near, after):
    per_dev, width = normed_rows.shape
    units = 2 * shard
    where = dict(places, pieces=places["near" if near else "far"])
    whole = lambda shape: pl.BlockSpec(shape, lambda i, t, c: (0,) * len(shape))
    return pl.pallas_call(
        functools.partial(chunk_kernel, where, len(pieces), len(after)),
        grid_spec=pltpu.PrefetchScalarGridSpec(
            num_scalar_prefetch=2,
            grid=(1,),
            in_specs=[
                whole((per_dev, width)),
                pl.BlockSpec((per_dev, units), lambda i, t, c: (0, t[places["chunk"] + step])),
                whole((1, units)),
            ]
            + [whole(p.shape) for p in pieces]
            + [pl.BlockSpec(memory_space=pl.ANY)] * len(after),
            out_specs=[
                whole((units // 2, width)),
                whole((units // 4, width)),
                whole((units // 4, width)),
                whole((per_dev, units)),
                whole((units, width)),
            ],
            scratch_shapes=[pltpu.VMEM((units, width), F32)],
        ),
        out_shape=[
            jax.ShapeDtypeStruct((units // 2, width), BF16),
            jax.ShapeDtypeStruct((units // 4, width), BF16),
            jax.ShapeDtypeStruct((units // 4, width), BF16),
            jax.ShapeDtypeStruct((per_dev, units), BF16),
            jax.ShapeDtypeStruct((units, width), BF16),
        ],
        compiler_params=pltpu.CompilerParams(vmem_limit_bytes=LIMIT),
        cost_estimate=pl.CostEstimate(
            flops=80 * per_dev * units * width,
            bytes_accessed=2 * per_dev * (width + 2 * units) + 6 * units * width,
            transcendentals=per_dev * units,
        ),
        name="chunk_%d" % step,
    )(table, counts, normed_rows, grad_hidden, bias, *pieces, *after)


def fast_device(plan, rows, grad_hidden, counts, w_in, b_in, gamma, beta):
    per_dev, width = rows.shape
    shard, quarter = plan.shard, plan.quarter
    n_patch = plan.n_patch
    dp_index, patch_index = lax.axis_index("dp"), lax.axis_index("patch")
    places = plan.places()
    table = lax.dynamic_index_in_dim(
        jnp.asarray(plan.table()), dp_index * n_patch + patch_index, 0, keepdims=False
    )
    swap = lambda to: functools.partial(lax.ppermute, axis_name=AXES, perm=plan.perm(to))
    core = swap(lambda x, c, z, y: (x, 1 - c, z, y))
    along_x = swap(lambda x, c, z, y: (1 - x, c, z, y))
    along_y = swap(lambda x, c, z, y: (x, c, z, 1 - y))
    first, second = swap(plan.first), swap(plan.second)
    up = lambda s: swap(lambda x, c, z, y: (x, c, (z + s) % plan.nz, y))
    half = per_dev // 2
    tile = half // 2

    units = 2 * shard
    bias = b_in.reshape(1, shard)
    low = patch_index % 2 == 0
    place = lambda row: jnp.where(
        low, jnp.pad(row, ((0, 0), (0, width - shard))), jnp.pad(row, ((0, 0), (shard, width - units)))
    )
    in_quarter = lax.broadcasted_iota(jnp.int32, (1, shard), 1) // quarter == dp_index
    bias_row = jnp.broadcast_to(place(jnp.where(in_quarter, bias, jnp.zeros((), BF16))), (8, width))
    mine = jnp.concatenate([lax.dynamic_slice_in_dim(w_in, dp_index * quarter, quarter, 0), bias_row], axis=0)
    bias_own = place(bias)[:, :units]

    from_z = {s: up(s)(mine) for s in (1, plan.nz - 1)}
    beside = along_y(mine)
    normed_rows = pl.pallas_call(
        norm_kernel,
        grid=(per_dev // tile,),
        in_specs=[
            pl.BlockSpec((tile, width), lambda i: (i, 0)),
            pl.BlockSpec((width,), lambda i: (0,)),
            pl.BlockSpec((width,), lambda i: (0,)),
        ],
        out_specs=pl.BlockSpec((tile, width), lambda i: (i, 0)),
        out_shape=jax.ShapeDtypeStruct((per_dev, width), BF16),
        compiler_params=pltpu.CompilerParams(vmem_limit_bytes=LIMIT),
        name="norm",
    )(rows, gamma, beta)
    beside, normed_rows = lax.optimization_barrier((beside, normed_rows))
    for s in range(2, plan.nz - 1):
        from_z[s] = up(1)(from_z[s - 1])
    diagonal = along_x(beside)
    pieces = {0: [w_in, beside, diagonal, core(beside), core(diagonal)]}
    order = [0, 1, plan.nz - 1] + list(range(2, plan.nz - 1)) if plan.nz > 2 else [0, 1]
    for s in order[1:]:
        a0 = from_z[s]
        a1 = first(a0)
        a2, a3 = second(a0), second(a1)
        pieces[s] = [a0, a1, a2, a3] + [core(a) for a in (a0, a1, a2, a3)]

    cut = lambda array, at, n=1: array[at * quarter : (at + n) * quarter].astype(F32)
    tied = lambda array, gate: lax.optimization_barrier((array, *gate))[0]

    def homeward(s, keep, send_first, send_second):
        got_first, got_second = core(send_first), core(send_second)
        gate = yield None
        got_first = tied(got_first, gate)
        t = (cut(keep, 0, 2) + got_first.astype(F32)).astype(BF16)
        gate = yield t
        one = tied(first(t), gate)
        v = (cut(keep, 2) + cut(got_second, 0) + cut(one, 0)).astype(BF16)
        gate = yield v
        two = tied(second(v), gate)
        plane = cut(keep, 3) + cut(got_second, 1) + cut(one, 1) + two.astype(F32)
        plane = plane if s == 0 else plane.astype(BF16)
        gate = yield plane
        term = plane if s == 0 else tied(up(-s)(plane), gate or [])
        while True:
            yield term

    def advance(gate=(), last=4):
        gate = list(gate)
        for at, m in enumerate(moving):
            if steps[at] < last:
                gate = [m.send(gate)]
                steps[at] += 1
        return gate

    hidden, weights, moving, steps = [], [], [], []
    empty = jnp.zeros((1, units), BF16)
    after = [from_z[s] for s in order[1:]]
    for s in order:
        keep, send_first, send_second, h, w = call_chunk(
            places, s, table, counts, normed_rows, grad_hidden, bias_own if s == 0 else empty, pieces[s], shard,
            s == 0, after,
        )
        hidden.append(h)
        weights.append(w)
        moving.append(homeward(s, keep, send_first, send_second))
        next(moving[-1])
        steps.append(0)
        after = advance()

    def call_rows(part, after, out):
        whole = lambda shape: pl.BlockSpec(shape, lambda i, t, c: (0,) * len(shape))
        striped = lambda cols: pl.BlockSpec((tile, cols), lambda i, t, c: (i + 2 * part, 0))
        more = list(after) + list(out)
        return pl.pallas_call(
            functools.partial(rows_kernel, places, plan.nz, 2 * part),
            grid_spec=pltpu.PrefetchScalarGridSpec(
                num_scalar_prefetch=2,
                grid=(2,),
                in_specs=[striped(width), pl.BlockSpec((width,), lambda i, t, c: (0,))]
                + [striped(h.shape[1]) for h in hidden]
                + [whole(w.shape) for w in weights]
                + [pl.BlockSpec(memory_space=pl.ANY)] * len(more),
                out_specs=striped(width),
            ),
            out_shape=jax.ShapeDtypeStruct((per_dev, width), BF16),
            input_output_aliases={3 + 2 * plan.nz + len(more): 0} if out else {},
            compiler_params=pltpu.CompilerParams(vmem_limit_bytes=LIMIT),
            cost_estimate=pl.CostEstimate(
                flops=40 * half * width * units * plan.nz,
                bytes_accessed=4 * half * width + 2 * (half + width) * units * plan.nz,
                transcendentals=0,
            ),
            name="grad_rows_%d" % part,
        )(table, counts, rows, gamma, *hidden, *weights, *more)

    grad_rows = call_rows(0, after, [])
    after = [grad_rows]
    while min(steps) < 3:
        after = advance(after, 3)
    grad_rows = call_rows(1, after, [grad_rows])
    scale = 1.0 / math.sqrt(VIS_DEV * n_patch * 4)
    total = sum(next(m).astype(F32) for m in moving)
    total, grad_rows = lax.optimization_barrier((total, grad_rows))
    done = (total * scale).astype(BF16)
    done_x = along_x(done)
    quarters = [done, done_x, core(done), core(done_x)]
    grad_w_in = pl.pallas_call(
        functools.partial(place_kernel, places),
        in_specs=[SMEM] + [VMEM] * 4,
        out_specs=VMEM,
        out_shape=jax.ShapeDtypeStruct((shard, width), F32),
        name="place",
    )(table, *quarters)
    return grad_rows, grad_w_in


def any_device(rows, grad_hidden, counts, w_in, b_in, gamma, beta):
    patch_count, data_count = lax.axis_size("patch"), lax.axis_size("dp")
    live = (jnp.arange(rows.shape[0], dtype=jnp.int32) < jnp.take(counts[0], lax.axis_index("patch")))[:, None]
    standard, inverse = standardise(rows)
    normed_rows = (standard * gamma + beta).astype(BF16)
    w_all = lax.all_gather(w_in, "patch", axis=0, tiled=True)
    b_all = lax.all_gather(b_in, "patch", axis=0, tiled=True)
    pre_act = lax.dot_general(normed_rows, w_all, (((1,), (1,)), ((), ())), preferred_element_type=F32)
    slope = gelu_slope(pre_act + b_all.astype(F32))
    hidden = jnp.where(live, grad_hidden.astype(F32) * slope, 0.0).astype(BF16)
    scaled = jnp.dot(hidden, w_all, preferred_element_type=F32) * gamma
    first = jnp.mean(scaled, axis=1, keepdims=True)
    second = jnp.mean(scaled * standard, axis=1, keepdims=True)
    grad = inverse * (scaled - first - standard * second)
    grad_rows = jnp.where(live, grad, 0.0).astype(BF16)
    term = lax.dot_general(hidden, normed_rows, (((0,), (0,)), ((), ())), preferred_element_type=F32)
    scale = 1.0 / math.sqrt(VIS_DEV * patch_count * data_count)
    part = lax.psum_scatter(term * scale, "patch", scatter_dimension=0, tiled=True)
    return grad_rows, lax.psum(part, "dp")


def solution(mesh):
    n_dp, n_patch = mesh.shape["dp"], mesh.shape["patch"]

    def per_device(*args):
        shard = args[3].shape[0]
        if n_dp == 4 and n_patch % 2 == 0 and n_patch <= 8 and shard % 64 == 0 and args[0].shape[0] % 64 == 0:
            return fast_device(Plan(n_dp, n_patch, shard), *args)
        return any_device(*args)

    in_specs = (
        P(AXES, None), P(AXES, None), P("dp", None), P("patch", None), P("patch"), P(), P(),
    )
    return jax.shard_map(
        per_device, mesh=mesh, in_specs=in_specs, out_specs=(P(AXES, None), P("patch", None)), check_vma=False
    )
```

```python
import functools
import math

import jax
import jax.numpy as jnp
import numpy as np
from jax import lax
from jax.experimental import pallas as pl
from jax.experimental.pallas import tpu as pltpu
from jax.sharding import PartitionSpec as P

VIS_DEV = 352
AXES = ("dp", "patch")
F32, BF16 = jnp.float32, jnp.bfloat16
VMEM = pl.BlockSpec(memory_space=pltpu.VMEM)
SMEM = pl.BlockSpec(memory_space=pltpu.SMEM)
LIMIT = 30 * 1024 * 1024


def gelu_slope(pre_act):
    normal_cdf = 0.5 * (1.0 + lax.erf(pre_act * (1.0 / math.sqrt(2.0))))
    density = jnp.exp(-0.5 * pre_act * pre_act) * (1.0 / math.sqrt(2.0 * math.pi))
    return normal_cdf + pre_act * density


def standardise(block):
    as_float = block.astype(F32)
    mean_row = jnp.mean(as_float, axis=1, keepdims=True)
    centred = as_float - mean_row
    variance = jnp.mean(centred * centred, axis=1, keepdims=True)
    inverse = lax.rsqrt(variance + 1e-05)
    return centred * inverse, inverse


def norm_kernel(rows_ref, gamma_ref, beta_ref, out_ref):
    standard, _ = standardise(rows_ref[...])
    out_ref[...] = (standard * gamma_ref[...].reshape(1, -1) + beta_ref[...].reshape(1, -1)).astype(BF16)


def chunk_kernel(places, pieces, waits, table_ref, counts_ref, n_ref, g_ref, b_ref, *refs):
    piece_refs, (keep_ref, *send_refs, h_ref, w_ref), (sum_ref,) = (
        refs[:pieces],
        refs[pieces + waits : pieces + waits + 7],
        refs[pieces + waits + 7 :],
    )
    block = keep_ref.shape[0] // 4
    bias = b_ref[...].astype(F32)
    for at, piece in enumerate(piece_refs):
        start = pl.multiple_of(table_ref[places["pieces"] + at], 16)
        extra = piece.shape[0] % block
        size = piece.shape[0] - extra
        w_ref[pl.ds(start, size), :] = piece[:size, :]
        if extra:
            bias += piece[size:, : bias.shape[1]].astype(F32)[:1]
    per_dev, units = h_ref.shape
    count = counts_ref[0, table_ref[places["patch"]]]
    live = lax.broadcasted_iota(jnp.int32, (per_dev, 1), 0) < count
    for low in range(0, units, 256):
        cols = slice(low, min(low + 256, units))
        pre_act = lax.dot_general(n_ref[...], w_ref[cols, :], (((1,), (1,)), ((), ())), preferred_element_type=F32)
        slope = gelu_slope(pre_act + bias[:, cols])
        hidden = jnp.where(live, g_ref[:, cols].astype(F32) * slope, 0.0)
        h_ref[:, cols] = hidden.astype(BF16)
    width = n_ref.shape[1]
    for low in range(0, width, 256):
        cols = slice(low, min(low + 256, width))
        sum_ref[:, cols] = lax.dot_general(
            h_ref[...], n_ref[:, cols], (((0,), (0,)), ((), ())), preferred_element_type=F32
        )
    for at in range(8):
        start = pl.multiple_of(table_ref[places["blocks"] + at], 16)
        out, to = (send_refs[at], 0) if at < 4 else (keep_ref, at % 4)
        out[to * block : (to + 1) * block, :] = sum_ref[pl.ds(start, block), :].astype(BF16)


def rows_kernel(places, chunks, first_tile, table_ref, counts_ref, rows_ref, gamma_ref, *refs):
    h_refs, w_refs, out_ref = refs[:chunks], refs[chunks : 2 * chunks], refs[-1]
    tile = rows_ref.shape[0]
    normed_grad = jnp.dot(h_refs[0][...], w_refs[0][...], preferred_element_type=F32)
    for h, w in zip(h_refs[1:], w_refs[1:]):
        normed_grad += jnp.dot(h[...], w[...], preferred_element_type=F32)
    standard, inverse = standardise(rows_ref[...])
    scaled = normed_grad * gamma_ref[...].reshape(1, -1)
    first = jnp.mean(scaled, axis=1, keepdims=True)
    second = jnp.mean(scaled * standard, axis=1, keepdims=True)
    grad = inverse * (scaled - first - standard * second)
    count = counts_ref[0, table_ref[places["patch"]]]
    row = lax.broadcasted_iota(jnp.int32, (tile, 1), 0) + (pl.program_id(0) + first_tile) * tile
    out_ref[...] = jnp.where(row < count, grad, 0.0).astype(BF16)


def place_kernel(places, table_ref, *refs):
    quarter = refs[0].shape[0]
    for at, piece in enumerate(refs[:-1]):
        start = pl.multiple_of(table_ref[places["final"] + at], 16)
        refs[-1][pl.ds(start, quarter), :] = piece[...].astype(F32)


class Plan:
    def __init__(self, n_dp, n_patch, shard):
        self.nz, self.ny, self.nx = n_patch // 2, 2, 2
        self.n_patch, self.shard, self.quarter = n_patch, shard, shard // 4
        self.everyone = [
            (x, c, z, y) for x in range(2) for c in range(2) for z in range(self.nz) for y in range(2)
        ]

    def lin(self, x, c, z, y):
        return ((x * 2 + c) * self.nz + z) * 2 + y

    def perm(self, to):
        return [(self.lin(*d), self.lin(*to(*d))) for d in self.everyone]

    def across(self, x, c, z, y, flip_x, flip_y):
        return (x ^ flip_x, c, z, y ^ flip_y)

    def first(self, x, c, z, y):
        return (1 - x, c, z, y) if c == 0 else (x, c, z, 1 - y)

    def second(self, x, c, z, y):
        return (1 - x, c, z, y) if c == 1 else (x, c, z, 1 - y)

    def row(self, x, c, z, y):
        return y * self.shard + (x * 2 + c) * self.quarter

    def table(self):
        rows = []
        for d in self.everyone:
            x, c, z, y = d
            twin = (x, 1 - c, z, y)
            four = lambda e: [e, self.first(*e), self.second(*e), self.second(*self.first(*e))]
            order = lambda e: [four(e)[i] for i in (3, 1, 2, 0)]
            entry = [z * 2 + y]
            entry += [(z - s) % self.nz for s in range(self.nz)]
            entry += [self.row(*e) for e in four(d) + four(twin)]
            entry += [y * self.shard] + [
                self.row(qx, qc, z, 1 - y) for qx, qc in ((x, c), (1 - x, c), (x, 1 - c), (1 - x, 1 - c))
            ]
            entry += [self.row(*e) for e in order(twin) + order(d)]
            entry += [
                self.row(qx, qc, z, 0) for qx, qc in ((x, c), (1 - x, c), (x, 1 - c), (1 - x, 1 - c))
            ]
            rows.append(entry)
        return np.array(rows, np.int32)

    def places(self):
        base = 1 + self.nz
        return {"patch": 0, "chunk": 1, "far": base, "near": base + 8, "blocks": base + 13, "final": base + 21}


def call_chunk(places, step, table, counts, normed_rows, grad_hidden, bias, pieces, shard, near, after):
    per_dev, width = normed_rows.shape
    units = 2 * shard
    where = dict(places, pieces=places["near" if near else "far"])
    whole = lambda shape: pl.BlockSpec(shape, lambda i, t, c: (0,) * len(shape))
    return pl.pallas_call(
        functools.partial(chunk_kernel, where, len(pieces), len(after)),
        grid_spec=pltpu.PrefetchScalarGridSpec(
            num_scalar_prefetch=2,
            grid=(1,),
            in_specs=[
                whole((per_dev, width)),
                pl.BlockSpec((per_dev, units), lambda i, t, c: (0, t[places["chunk"] + step])),
                whole((1, units)),
            ]
            + [whole(p.shape) for p in pieces]
            + [pl.BlockSpec(memory_space=pl.ANY)] * len(after),
            out_specs=[
                whole((units // 2, width)),
                *[whole((units // 8, width))] * 4,
                whole((per_dev, units)),
                whole((units, width)),
            ],
            scratch_shapes=[pltpu.VMEM((units, width), F32)],
        ),
        out_shape=[
            jax.ShapeDtypeStruct((units // 2, width), BF16),
            *[jax.ShapeDtypeStruct((units // 8, width), BF16)] * 4,
            jax.ShapeDtypeStruct((per_dev, units), BF16),
            jax.ShapeDtypeStruct((units, width), BF16),
        ],
        compiler_params=pltpu.CompilerParams(vmem_limit_bytes=LIMIT),
        cost_estimate=pl.CostEstimate(
            flops=per_dev * units,
            bytes_accessed=0,
            transcendentals=0,
        ),
        name="chunk_%d" % step,
    )(table, counts, normed_rows, grad_hidden, bias, *pieces, *after)


def fast_device(plan, rows, grad_hidden, counts, w_in, b_in, gamma, beta):
    per_dev, width = rows.shape
    shard, quarter = plan.shard, plan.quarter
    n_patch = plan.n_patch
    dp_index, patch_index = lax.axis_index("dp"), lax.axis_index("patch")
    places = plan.places()
    table = lax.dynamic_index_in_dim(
        jnp.asarray(plan.table()), dp_index * n_patch + patch_index, 0, keepdims=False
    )
    swap = lambda to: functools.partial(lax.ppermute, axis_name=AXES, perm=plan.perm(to))
    core = swap(lambda x, c, z, y: (x, 1 - c, z, y))
    along_x = swap(lambda x, c, z, y: (1 - x, c, z, y))
    along_y = swap(lambda x, c, z, y: (x, c, z, 1 - y))
    first, second = swap(plan.first), swap(plan.second)
    up = lambda s: swap(lambda x, c, z, y: (x, c, (z + s) % plan.nz, y))
    half = per_dev // 2
    tile = half // 2

    units = 2 * shard
    bias = b_in.reshape(1, shard)
    low = patch_index % 2 == 0
    place = lambda row: jnp.where(
        low, jnp.pad(row, ((0, 0), (0, width - shard))), jnp.pad(row, ((0, 0), (shard, width - units)))
    )
    in_quarter = lax.broadcasted_iota(jnp.int32, (1, shard), 1) // quarter == dp_index
    bias_row = jnp.broadcast_to(place(jnp.where(in_quarter, bias, jnp.zeros((), BF16))), (8, width))
    mine = jnp.concatenate([lax.dynamic_slice_in_dim(w_in, dp_index * quarter, quarter, 0), bias_row], axis=0)
    bias_own = place(bias)[:, :units]

    from_z = {s: up(s)(mine) for s in (1, plan.nz - 1)}
    beside = along_y(mine)
    normed_rows = pl.pallas_call(
        norm_kernel,
        grid=(per_dev // tile,),
        in_specs=[
            pl.BlockSpec((tile, width), lambda i: (i, 0)),
            pl.BlockSpec((width,), lambda i: (0,)),
            pl.BlockSpec((width,), lambda i: (0,)),
        ],
        out_specs=pl.BlockSpec((tile, width), lambda i: (i, 0)),
        out_shape=jax.ShapeDtypeStruct((per_dev, width), BF16),
        compiler_params=pltpu.CompilerParams(vmem_limit_bytes=LIMIT),
        name="norm",
    )(rows, gamma, beta)
    tied = lambda array, gate: lax.optimization_barrier((array, *gate))[0]
    from_z[2] = up(1)(from_z[1])
    from_z[1] = tied(from_z[1], [from_z[3], normed_rows])
    diagonal = along_x(beside)
    pieces = {0: [w_in, beside, diagonal, core(beside), core(diagonal)]}
    arrival = [1, 3, 2]
    for s in arrival:
        a0 = from_z[s]
        a1 = first(a0)
        a2, a3 = second(a0), second(a1)
        pieces[s] = [a0, a1, a2, a3] + [core(a) for a in (a0, a1, a2, a3)]

    cut = lambda array, at, n=1: array[at * quarter : (at + n) * quarter].astype(F32)

    def homeward(s, keep, *sends):
        got = [core(send) for send in sends]
        gate = yield None
        got[0] = tied(got[0], gate)
        t = (cut(keep, 0, 2) + jnp.concatenate(got[:2], axis=0).astype(F32)).astype(BF16)
        gate = yield t
        one = tied(first(t), gate)
        v = (cut(keep, 2) + got[2].astype(F32) + cut(one, 0)).astype(BF16)
        gate = yield v
        two = tied(second(v), gate)
        plane = cut(keep, 3) + got[3].astype(F32) + cut(one, 1) + two.astype(F32)
        plane = plane if s == 0 else plane.astype(BF16)
        gate = yield plane
        term = plane if s == 0 else tied(up(-s)(plane), gate or [])
        while True:
            yield term

    def advance(steps, gate=()):
        gate = list(gate)
        for at in steps:
            gate = [moving[at].send(gate)]
        return gate

    hidden, weights, moving = [], [], []
    empty = jnp.zeros((1, units), BF16)
    order = [0] + arrival
    after = []
    for at, s in enumerate(order):
        keep, *sends, h, w = call_chunk(
            places, s, tied(table, after + [[from_z[2]],[],[],[]][at]), counts, normed_rows, grad_hidden, bias_own if s == 0 else empty,
            pieces[s], shard, s == 0, [],
        )
        hidden.append(h)
        weights.append(w)
        moving.append(homeward(s, keep, *sends))
        next(moving[-1])
        after = advance([[0],[0,1],[0,1,2],[1,2,3],[1,2,3],[3]][at])

    def call_rows(part, after, out):
        whole = lambda shape: pl.BlockSpec(shape, lambda i, t, c: (0,) * len(shape))
        striped = lambda cols: pl.BlockSpec((tile, cols), lambda i, t, c: (i + 2 * part, 0))
        more = list(out)
        return pl.pallas_call(
            functools.partial(rows_kernel, places, plan.nz, 2 * part),
            grid_spec=pltpu.PrefetchScalarGridSpec(
                num_scalar_prefetch=2,
                grid=(2,),
                in_specs=[striped(width), pl.BlockSpec((width,), lambda i, t, c: (0,))]
                + [striped(h.shape[1]) for h in hidden]
                + [whole(w.shape) for w in weights]
                + [pl.BlockSpec(memory_space=pl.ANY)] * len(more),
                out_specs=striped(width),
            ),
            out_shape=jax.ShapeDtypeStruct((per_dev, width), BF16),
            input_output_aliases={3 + 2 * plan.nz + len(more): 0} if out else {},
            compiler_params=pltpu.CompilerParams(vmem_limit_bytes=LIMIT),
            cost_estimate=pl.CostEstimate(
                flops=half * width,
                bytes_accessed=0,
                transcendentals=0,
            ),
            name="grad_rows_%d" % part,
        )(tied(table, after), counts, rows, gamma, *hidden, *weights, *more)

    grad_rows = call_rows(0, after, [])
    after = [grad_rows]
    for steps in [[0],[0,1],[0,1,2],[1,2,3],[1,2,3],[3]][4:]:
        after = advance(steps, after)
    grad_rows = call_rows(1, after, [grad_rows])
    scale = 1.0 / math.sqrt(VIS_DEV * n_patch * 4)
    total = sum(next(m).astype(F32) for m in moving)
    total, grad_rows = lax.optimization_barrier((total, grad_rows))
    done = (total * scale).astype(BF16)
    done_x = along_x(done)
    quarters = [done, done_x, core(done), core(done_x)]
    same_x, same_c = [dp_index // 2 == v for v in (0, 1)], [dp_index % 2 == v for v in (0, 1)]
    grad_w_in = jnp.concatenate(
        [
            jnp.where(
                same_x[at // 2],
                jnp.where(same_c[at % 2], quarters[0], quarters[2]),
                jnp.where(same_c[at % 2], quarters[1], quarters[3]),
            ).astype(F32)
            for at in range(4)
        ],
        axis=0,
    )
    return grad_rows, grad_w_in


def any_device(rows, grad_hidden, counts, w_in, b_in, gamma, beta):
    patch_count, data_count = lax.axis_size("patch"), lax.axis_size("dp")
    live = (jnp.arange(rows.shape[0], dtype=jnp.int32) < jnp.take(counts[0], lax.axis_index("patch")))[:, None]
    standard, inverse = standardise(rows)
    normed_rows = (standard * gamma + beta).astype(BF16)
    w_all = lax.all_gather(w_in, "patch", axis=0, tiled=True)
    b_all = lax.all_gather(b_in, "patch", axis=0, tiled=True)
    pre_act = lax.dot_general(normed_rows, w_all, (((1,), (1,)), ((), ())), preferred_element_type=F32)
    slope = gelu_slope(pre_act + b_all.astype(F32))
    hidden = jnp.where(live, grad_hidden.astype(F32) * slope, 0.0).astype(BF16)
    scaled = jnp.dot(hidden, w_all, preferred_element_type=F32) * gamma
    first = jnp.mean(scaled, axis=1, keepdims=True)
    second = jnp.mean(scaled * standard, axis=1, keepdims=True)
    grad = inverse * (scaled - first - standard * second)
    grad_rows = jnp.where(live, grad, 0.0).astype(BF16)
    term = lax.dot_general(hidden, normed_rows, (((0,), (0,)), ((), ())), preferred_element_type=F32)
    scale = 1.0 / math.sqrt(VIS_DEV * patch_count * data_count)
    part = lax.psum_scatter(term * scale, "patch", scatter_dimension=0, tiled=True)
    return grad_rows, lax.psum(part, "dp")


def solution(mesh):
    n_dp, n_patch = mesh.shape["dp"], mesh.shape["patch"]

    def per_device(*args):
        shard = args[3].shape[0]
        if n_dp == 4 and n_patch == 8 and shard % 64 == 0 and args[0].shape[0] % 64 == 0:
            return fast_device(Plan(n_dp, n_patch, shard), *args)
        return any_device(*args)

    in_specs = (
        P(AXES, None), P(AXES, None), P("dp", None), P("patch", None), P("patch"), P(), P(),
    )
    return jax.shard_map(
        per_device, mesh=mesh, in_specs=in_specs, out_specs=(P(AXES, None), P("patch", None)), check_vma=False
    )
```

```python
import functools
import math

import jax
import jax.numpy as jnp
import numpy as np
from jax import lax
from jax.experimental import pallas as pl
from jax.experimental.pallas import tpu as pltpu
from jax.sharding import PartitionSpec as P

VIS_DEV = 352
AXES = ("dp", "patch")
F32, BF16 = jnp.float32, jnp.bfloat16
VMEM = pl.BlockSpec(memory_space=pltpu.VMEM)
SMEM = pl.BlockSpec(memory_space=pltpu.SMEM)
LIMIT = 30 * 1024 * 1024


def gelu_slope(pre_act):
    normal_cdf = 0.5 * (1.0 + lax.erf(pre_act * (1.0 / math.sqrt(2.0))))
    density = jnp.exp(-0.5 * pre_act * pre_act) * (1.0 / math.sqrt(2.0 * math.pi))
    return normal_cdf + pre_act * density


def standardise(block):
    as_float = block.astype(F32)
    mean_row = jnp.mean(as_float, axis=1, keepdims=True)
    centred = as_float - mean_row
    variance = jnp.mean(centred * centred, axis=1, keepdims=True)
    inverse = lax.rsqrt(variance + 1e-05)
    return centred * inverse, inverse


def norm_kernel(rows_ref, gamma_ref, beta_ref, out_ref):
    standard, _ = standardise(rows_ref[...])
    out_ref[...] = (standard * gamma_ref[...].reshape(1, -1) + beta_ref[...].reshape(1, -1)).astype(BF16)


def chunk_kernel(places, pieces, waits, table_ref, counts_ref, n_ref, g_ref, b_ref, *refs):
    piece_refs, (keep_ref, *send_refs, h_ref, w_ref), (sum_ref,) = (
        refs[:pieces],
        refs[pieces + waits : pieces + waits + 7],
        refs[pieces + waits + 7 :],
    )
    block = keep_ref.shape[0] // 4
    bias = b_ref[...].astype(F32)
    for at, piece in enumerate(piece_refs):
        start = pl.multiple_of(table_ref[places["pieces"] + at], 16)
        extra = piece.shape[0] % block
        size = piece.shape[0] - extra
        w_ref[pl.ds(start, size), :] = piece[:size, :]
        if extra:
            bias += piece[size:, : bias.shape[1]].astype(F32)[:1]
    per_dev, units = h_ref.shape
    count = counts_ref[0, table_ref[places["patch"]]]
    live = lax.broadcasted_iota(jnp.int32, (per_dev, 1), 0) < count
    for low in range(0, units, 256):
        cols = slice(low, min(low + 256, units))
        pre_act = lax.dot_general(n_ref[...], w_ref[cols, :], (((1,), (1,)), ((), ())), preferred_element_type=F32)
        slope = gelu_slope(pre_act + bias[:, cols])
        hidden = jnp.where(live, g_ref[:, cols].astype(F32) * slope, 0.0)
        h_ref[:, cols] = hidden.astype(BF16)
    width = n_ref.shape[1]
    for low in range(0, width, 256):
        cols = slice(low, min(low + 256, width))
        sum_ref[:, cols] = lax.dot_general(
            h_ref[...], n_ref[:, cols], (((0,), (0,)), ((), ())), preferred_element_type=F32
        )
    for at in range(8):
        start = pl.multiple_of(table_ref[places["blocks"] + at], 16)
        out, to = (send_refs[at], 0) if at < 4 else (keep_ref, at % 4)
        out[to * block : (to + 1) * block, :] = sum_ref[pl.ds(start, block), :].astype(BF16)


def rows_kernel(places, chunks, first_tile, table_ref, counts_ref, rows_ref, gamma_ref, *refs):
    h_refs, w_refs, out_ref = refs[:chunks], refs[chunks : 2 * chunks], refs[-1]
    tile = rows_ref.shape[0]
    normed_grad = jnp.dot(h_refs[0][...], w_refs[0][...], preferred_element_type=F32)
    for h, w in zip(h_refs[1:], w_refs[1:]):
        normed_grad += jnp.dot(h[...], w[...], preferred_element_type=F32)
    standard, inverse = standardise(rows_ref[...])
    scaled = normed_grad * gamma_ref[...].reshape(1, -1)
    first = jnp.mean(scaled, axis=1, keepdims=True)
    second = jnp.mean(scaled * standard, axis=1, keepdims=True)
    grad = inverse * (scaled - first - standard * second)
    count = counts_ref[0, table_ref[places["patch"]]]
    row = lax.broadcasted_iota(jnp.int32, (tile, 1), 0) + (pl.program_id(0) + first_tile) * tile
    out_ref[...] = jnp.where(row < count, grad, 0.0).astype(BF16)


def place_kernel(places, table_ref, *refs):
    quarter = refs[0].shape[0]
    for at, piece in enumerate(refs[:-1]):
        start = pl.multiple_of(table_ref[places["final"] + at], 16)
        refs[-1][pl.ds(start, quarter), :] = piece[...].astype(F32)


class Plan:
    def __init__(self, n_dp, n_patch, shard):
        self.nz, self.ny, self.nx = n_patch // 2, 2, 2
        self.n_patch, self.shard, self.quarter = n_patch, shard, shard // 4
        self.everyone = [
            (x, c, z, y) for x in range(2) for c in range(2) for z in range(self.nz) for y in range(2)
        ]

    def lin(self, x, c, z, y):
        return ((x * 2 + c) * self.nz + z) * 2 + y

    def perm(self, to):
        return [(self.lin(*d), self.lin(*to(*d))) for d in self.everyone]

    def across(self, x, c, z, y, flip_x, flip_y):
        return (x ^ flip_x, c, z, y ^ flip_y)

    def first(self, x, c, z, y):
        return (1 - x, c, z, y) if c == 0 else (x, c, z, 1 - y)

    def second(self, x, c, z, y):
        return (1 - x, c, z, y) if c == 1 else (x, c, z, 1 - y)

    def row(self, x, c, z, y):
        return y * self.shard + (x * 2 + c) * self.quarter

    def table(self):
        rows = []
        for d in self.everyone:
            x, c, z, y = d
            twin = (x, 1 - c, z, y)
            four = lambda e: [e, self.first(*e), self.second(*e), self.second(*self.first(*e))]
            order = lambda e: [four(e)[i] for i in (3, 1, 2, 0)]
            entry = [z * 2 + y]
            entry += [(z - s) % self.nz for s in range(self.nz)]
            entry += [self.row(*e) for e in four(d) + four(twin)]
            entry += [y * self.shard] + [
                self.row(qx, qc, z, 1 - y) for qx, qc in ((x, c), (1 - x, c), (x, 1 - c), (1 - x, 1 - c))
            ]
            entry += [self.row(*e) for e in order(twin) + order(d)]
            entry += [
                self.row(qx, qc, z, 0) for qx, qc in ((x, c), (1 - x, c), (x, 1 - c), (1 - x, 1 - c))
            ]
            rows.append(entry)
        return np.array(rows, np.int32)

    def places(self):
        base = 1 + self.nz
        return {"patch": 0, "chunk": 1, "far": base, "near": base + 8, "blocks": base + 13, "final": base + 21}


def call_chunk(places, step, table, counts, normed_rows, grad_hidden, bias, pieces, shard, near, after):
    per_dev, width = normed_rows.shape
    units = 2 * shard
    where = dict(places, pieces=places["near" if near else "far"])
    whole = lambda shape: pl.BlockSpec(shape, lambda i, t, c: (0,) * len(shape))
    return pl.pallas_call(
        functools.partial(chunk_kernel, where, len(pieces), len(after)),
        grid_spec=pltpu.PrefetchScalarGridSpec(
            num_scalar_prefetch=2,
            grid=(1,),
            in_specs=[
                whole((per_dev, width)),
                pl.BlockSpec((per_dev, units), lambda i, t, c: (0, t[places["chunk"] + step])),
                whole((1, units)),
            ]
            + [whole(p.shape) for p in pieces]
            + [pl.BlockSpec(memory_space=pl.ANY)] * len(after),
            out_specs=[
                whole((units // 2, width)),
                *[whole((units // 8, width))] * 4,
                whole((per_dev, units)),
                whole((units, width)),
            ],
            scratch_shapes=[pltpu.VMEM((units, width), F32)],
        ),
        out_shape=[
            jax.ShapeDtypeStruct((units // 2, width), BF16),
            *[jax.ShapeDtypeStruct((units // 8, width), BF16)] * 4,
            jax.ShapeDtypeStruct((per_dev, units), BF16),
            jax.ShapeDtypeStruct((units, width), BF16),
        ],
        compiler_params=pltpu.CompilerParams(vmem_limit_bytes=LIMIT),
        cost_estimate=pl.CostEstimate(
            flops=per_dev * units,
            bytes_accessed=0,
            transcendentals=0,
        ),
        name="chunk_%d" % step,
    )(table, counts, normed_rows, grad_hidden, bias, *pieces, *after)


def fast_device(plan, rows, grad_hidden, counts, w_in, b_in, gamma, beta):
    per_dev, width = rows.shape
    shard, quarter = plan.shard, plan.quarter
    n_patch = plan.n_patch
    dp_index, patch_index = lax.axis_index("dp"), lax.axis_index("patch")
    places = plan.places()
    table = lax.dynamic_index_in_dim(
        jnp.asarray(plan.table()), dp_index * n_patch + patch_index, 0, keepdims=False
    )
    swap = lambda to: functools.partial(lax.ppermute, axis_name=AXES, perm=plan.perm(to))
    core = swap(lambda x, c, z, y: (x, 1 - c, z, y))
    along_x = swap(lambda x, c, z, y: (1 - x, c, z, y))
    along_y = swap(lambda x, c, z, y: (x, c, z, 1 - y))
    first, second = swap(plan.first), swap(plan.second)
    up = lambda s: swap(lambda x, c, z, y: (x, c, (z + s) % plan.nz, y))
    half = per_dev // 2
    tile = half // 2

    units = 2 * shard
    bias = b_in.reshape(1, shard)
    low = patch_index % 2 == 0
    place = lambda row: jnp.where(
        low, jnp.pad(row, ((0, 0), (0, width - shard))), jnp.pad(row, ((0, 0), (shard, width - units)))
    )
    in_quarter = lax.broadcasted_iota(jnp.int32, (1, shard), 1) // quarter == dp_index
    bias_row = jnp.broadcast_to(place(jnp.where(in_quarter, bias, jnp.zeros((), BF16))), (8, width))
    mine = jnp.concatenate([lax.dynamic_slice_in_dim(w_in, dp_index * quarter, quarter, 0), bias_row], axis=0)
    bias_own = place(bias)[:, :units]

    from_z = {s: up(s)(mine) for s in (1, plan.nz - 1)}
    beside = along_y(mine)
    normed_rows = pl.pallas_call(
        norm_kernel,
        grid=(per_dev // tile,),
        in_specs=[
            pl.BlockSpec((tile, width), lambda i: (i, 0)),
            pl.BlockSpec((width,), lambda i: (0,)),
            pl.BlockSpec((width,), lambda i: (0,)),
        ],
        out_specs=pl.BlockSpec((tile, width), lambda i: (i, 0)),
        out_shape=jax.ShapeDtypeStruct((per_dev, width), BF16),
        compiler_params=pltpu.CompilerParams(vmem_limit_bytes=LIMIT),
        name="norm",
    )(rows, gamma, beta)
    tied = lambda array, gate: lax.optimization_barrier((array, *gate))[0]
    from_z[2] = up(1)(from_z[1])
    from_z[1] = tied(from_z[1], [from_z[3], normed_rows])
    diagonal = along_x(beside)
    pieces = {0: [w_in, beside, diagonal, core(beside), core(diagonal)]}
    arrival = [3, 1, 2]
    for s in arrival:
        a0 = from_z[s]
        a1 = first(a0)
        a2, a3 = second(a0), second(a1)
        pieces[s] = [a0, a1, a2, a3] + [core(a) for a in (a0, a1, a2, a3)]

    cut = lambda array, at, n=1: array[at * quarter : (at + n) * quarter].astype(F32)

    def homeward(s, keep, *sends):
        got = [core(send) for send in sends]
        gate = yield None
        got[0] = tied(got[0], gate)
        t = (cut(keep, 0, 2) + jnp.concatenate(got[:2], axis=0).astype(F32)).astype(BF16)
        gate = yield t
        one = tied(first(t), gate)
        v = (cut(keep, 2) + got[2].astype(F32) + cut(one, 0)).astype(BF16)
        gate = yield v
        two = tied(second(v), gate)
        plane = cut(keep, 3) + got[3].astype(F32) + cut(one, 1) + two.astype(F32)
        plane = plane if s == 0 else plane.astype(BF16)
        gate = yield plane
        term = plane if s == 0 else tied(up(-s)(plane), gate or [])
        while True:
            yield term

    def advance(steps, gate=()):
        gate = list(gate)
        for at in steps:
            gate = [moving[at].send(gate)]
        return gate

    hidden, weights, moving = [], [], []
    empty = jnp.zeros((1, units), BF16)
    order = [0] + arrival
    after = []
    for at, s in enumerate(order):
        keep, *sends, h, w = call_chunk(
            places, s, tied(table, after + [[from_z[2]],[],[],[]][at]), counts, normed_rows, grad_hidden, bias_own if s == 0 else empty,
            pieces[s], shard, s == 0, [],
        )
        hidden.append(h)
        weights.append(w)
        moving.append(homeward(s, keep, *sends))
        next(moving[-1])
        after = advance([[0],[0,1],[0,2,1],[0,1,2,3],[1,2,3],[2,3]][at])

    def call_rows(part, after, out):
        whole = lambda shape: pl.BlockSpec(shape, lambda i, t, c: (0,) * len(shape))
        striped = lambda cols: pl.BlockSpec((tile, cols), lambda i, t, c: (i + 2 * part, 0))
        more = list(out)
        return pl.pallas_call(
            functools.partial(rows_kernel, places, plan.nz, 2 * part),
            grid_spec=pltpu.PrefetchScalarGridSpec(
                num_scalar_prefetch=2,
                grid=(2,),
                in_specs=[striped(width), pl.BlockSpec((width,), lambda i, t, c: (0,))]
                + [striped(h.shape[1]) for h in hidden]
                + [whole(w.shape) for w in weights]
                + [pl.BlockSpec(memory_space=pl.ANY)] * len(more),
                out_specs=striped(width),
            ),
            out_shape=jax.ShapeDtypeStruct((per_dev, width), BF16),
            input_output_aliases={3 + 2 * plan.nz + len(more): 0} if out else {},
            compiler_params=pltpu.CompilerParams(vmem_limit_bytes=LIMIT),
            cost_estimate=pl.CostEstimate(
                flops=half * width,
                bytes_accessed=0,
                transcendentals=0,
            ),
            name="grad_rows_%d" % part,
        )(tied(table, after), counts, rows, gamma, *hidden, *weights, *more)

    grad_rows = call_rows(0, after, [])
    after = [grad_rows]
    for steps in [[0],[0,1],[0,2,1],[0,1,2,3],[1,2,3],[2,3]][4:]:
        after = advance(steps, after)
    grad_rows = call_rows(1, after, [grad_rows])
    scale = 1.0 / math.sqrt(VIS_DEV * n_patch * 4)
    total = sum(next(m).astype(F32) for m in moving)
    total, grad_rows = lax.optimization_barrier((total, grad_rows))
    done = (total * scale).astype(BF16)
    done_x = along_x(done)
    quarters = [done, done_x, core(done), core(done_x)]
    same_x, same_c = [dp_index // 2 == v for v in (0, 1)], [dp_index % 2 == v for v in (0, 1)]
    grad_w_in = jnp.concatenate(
        [
            jnp.where(
                same_x[at // 2],
                jnp.where(same_c[at % 2], quarters[0], quarters[2]),
                jnp.where(same_c[at % 2], quarters[1], quarters[3]),
            ).astype(F32)
            for at in range(4)
        ],
        axis=0,
    )
    return grad_rows, grad_w_in


def any_device(rows, grad_hidden, counts, w_in, b_in, gamma, beta):
    patch_count, data_count = lax.axis_size("patch"), lax.axis_size("dp")
    live = (jnp.arange(rows.shape[0], dtype=jnp.int32) < jnp.take(counts[0], lax.axis_index("patch")))[:, None]
    standard, inverse = standardise(rows)
    normed_rows = (standard * gamma + beta).astype(BF16)
    w_all = lax.all_gather(w_in, "patch", axis=0, tiled=True)
    b_all = lax.all_gather(b_in, "patch", axis=0, tiled=True)
    pre_act = lax.dot_general(normed_rows, w_all, (((1,), (1,)), ((), ())), preferred_element_type=F32)
    slope = gelu_slope(pre_act + b_all.astype(F32))
    hidden = jnp.where(live, grad_hidden.astype(F32) * slope, 0.0).astype(BF16)
    scaled = jnp.dot(hidden, w_all, preferred_element_type=F32) * gamma
    first = jnp.mean(scaled, axis=1, keepdims=True)
    second = jnp.mean(scaled * standard, axis=1, keepdims=True)
    grad = inverse * (scaled - first - standard * second)
    grad_rows = jnp.where(live, grad, 0.0).astype(BF16)
    term = lax.dot_general(hidden, normed_rows, (((0,), (0,)), ((), ())), preferred_element_type=F32)
    scale = 1.0 / math.sqrt(VIS_DEV * patch_count * data_count)
    part = lax.psum_scatter(term * scale, "patch", scatter_dimension=0, tiled=True)
    return grad_rows, lax.psum(part, "dp")


def solution(mesh):
    n_dp, n_patch = mesh.shape["dp"], mesh.shape["patch"]

    def per_device(*args):
        shard = args[3].shape[0]
        if n_dp == 4 and n_patch == 8 and shard % 64 == 0 and args[0].shape[0] % 64 == 0:
            return fast_device(Plan(n_dp, n_patch, shard), *args)
        return any_device(*args)

    in_specs = (
        P(AXES, None), P(AXES, None), P("dp", None), P("patch", None), P("patch"), P(), P(),
    )
    return jax.shard_map(
        per_device, mesh=mesh, in_specs=in_specs, out_specs=(P(AXES, None), P("patch", None)), check_vma=False
    )
```
